256 devices in a mesh: wide: 32 (over y, z), narrow: 8 (over x, core).
Axes of the slice: x: 4, y: 4, z: 8, core: 2. Of those that a mesh axis runs over, the one named last changes fastest.
Arguments:
- cross_input: bfloat16 [32768, 3456], P(('wide', 'narrow')), may hold values from -6 to 6
- upstream: bfloat16 [32768, 3456], P(('wide', 'narrow')), may hold values from -6 to 6
- cross_down: bfloat16 [512, 3456], replicated, may hold values from -0.109375 to 0.109375
- cross_up: bfloat16 [512, 3456], replicated, may hold values from -0.25 to 0.25
- cross_bias: bfloat16 [3456], replicated, may hold values from -3 to 3
- bag_rows: int32 [32768, 26, 16], P(('wide', 'narrow')), may hold values from 0 to 511
- bag_lengths: int32 [32768, 26], P(('wide', 'narrow')), may hold values from 0 to 16
- table_owner: int32 [26], replicated, may hold values from 0 to 31, as said below
- table_rows: float32 [16384, 128], P('wide'), may hold values from -4 to 4
- row_accum: float32 [16384], P('wide'), may hold values from 20 to 600
- admitted: int32 [16384], P('wide'), may hold values 0 or 1
Outputs:
- new_rows: float32 [16384, 128], P('wide')
- new_accum: float32 [16384], P('wide')
- grad_up: float32 [512, 3456], P(('wide', 'narrow'))
- grad_down: float32 [512, 3456], P(('wide', 'narrow'))
The draws below stay inside these ranges and needn't reach their ends.
Inputs may be any that keep to these rules, and one draw needn't show every extreme that they name: `table_owner`: each wide index owns at most 2 tables, and some wide index owns exactly 2. `bag_rows`: ids at positions at or past a bag's length are arbitrary and unused.
All inputs are finite; a program needn't handle non-finite values. No bound on the sum of `admitted` on one device may be relied on, other than what follows from the above.
Results may differ from the reference program's by a relative error of at most 0.0041.
Values may be sent and summed in bfloat16 or wider, within the bound.
No kernel may reach another device: no remote copies, remote signals or barrier semaphores. Data moves between devices by JAX's collectives and lax.ppermute only.
A program may use at most 128 MiB of HBM per device.

```python
import math
import jax
import jax.numpy as jnp
from jax import lax

E = 128
NT = 26
R = 512
L = 16
UNQ = 512
F = 3456
SAMPLES = 32768
ROWS = 16384
TSLOT = 2
N_WIDE = 32


def draw_table_owner(key, part):
    key = jax.random.fold_in(key, 7)
    first, second, third = jax.random.split(key, 3)
    slot_total = N_WIDE * TSLOT
    scores = jax.random.permutation(first, slot_total).astype(jnp.int32)
    chosen = jax.random.randint(second, (), 0, N_WIDE)
    owner_of = jnp.arange(slot_total, dtype=jnp.int32) // TSLOT
    scores = jnp.where(owner_of == chosen, scores - slot_total, scores)
    ordering = jnp.argsort(scores, stable=True)
    owners = (ordering // TSLOT)[:NT]
    shuffle = jax.random.permutation(third, NT)
    return owners[shuffle].astype(jnp.int32)


def touch_ends(entries, key, smallest, high):
    place = [jax.random.randint(jax.random.fold_in(key, axis), (), 0, length) for axis, length in enumerate(entries.shape)]
    widest = entries.shape.index(max(entries.shape))
    beside = place[:widest] + [(place[widest] + 1) % entries.shape[widest]] + place[widest + 1:]
    return entries.at[tuple(place)].set(smallest).at[tuple(beside)].set(high)


def shard_levels(key, shape, shards, least, high):
    def one(dim, blocks):
        draws = jax.random.uniform(jax.random.fold_in(jax.random.fold_in(key, 6), dim), (blocks,), jnp.float32, least / len(shards), high / len(shards))
        return jnp.repeat(jnp.exp(draws), shape[dim] // blocks).reshape((-1,) + (1,) * (len(shape) - dim - 1))

    gain = one(*shards[0])
    for cut in shards[1:]:
        gain = gain * one(*cut)
    return gain


def noise(stream_key, dims, scale, bound, cuts=(), held_as=jnp.bfloat16):
    array = jax.random.normal(stream_key, dims, jnp.float32) * scale
    if len(cuts) > 0:
        array = shard_levels(stream_key, dims, cuts, -0.22, 0.18) * array
    return jnp.clip(array, min=-bound, max=bound).astype(held_as)


def setup_inputs(seed: int = 0) -> dict:
    splits = jax.random.split(jax.random.key(seed), 12)
    return {
        "cross_input": noise(splits[0], (SAMPLES, F), 1.0, 6.0, ((0, 256),)),
        "upstream": noise(splits[1], (SAMPLES, F), 1.0, 6.0, ((0, 256),)),
        "cross_down": noise(splits[2], (R, F), F ** -0.5, 0.109375),
        "cross_up": noise(splits[3], (R, F), R ** -0.5, 0.25),
        "cross_bias": noise(splits[4], (F,), 0.5, 3.0),
        "bag_rows": touch_ends(jax.random.randint(splits[5], (SAMPLES, NT, L), 0, UNQ), jax.random.fold_in(splits[5], 1), 0, UNQ - 1).astype(jnp.int32),
        "bag_lengths": touch_ends(jax.random.randint(splits[6], (SAMPLES, NT), 0, L + 1), jax.random.fold_in(splits[6], 1), 0, L).astype(jnp.int32),
        "table_owner": draw_table_owner(jax.random.fold_in(splits[11], 71), 0),
        "table_rows": noise(splits[8], (ROWS, E), 0.5, 4.0, ((0, 32),), jnp.float32),
        "row_accum": jnp.clip(jnp.exp(math.log(600.0) - 3.4011974 * jax.random.uniform(splits[9], (ROWS,), jnp.float32) ** shard_levels(splits[9], (ROWS,), ((0, 32),), -0.2, 0.2)), 20.0, 600.0),
        "admitted": touch_ends((jax.random.randint(splits[10], (ROWS,), 0, 4) < 1).astype(jnp.int32), jax.random.fold_in(splits[10], 1), 0, 1),
    }


def cross_backward(cross_input, upstream, cross_down, cross_up, cross_bias):
    low_rank = lax.dot_general(cross_input, cross_down, (((1,), (1,)), ((), ())), preferred_element_type=jnp.float32).astype(jnp.bfloat16)
    scale_c = jnp.dot(low_rank, cross_up, preferred_element_type=jnp.float32) + cross_bias.astype(jnp.float32)
    d_scale = (upstream.astype(jnp.float32) * cross_input.astype(jnp.float32)).astype(jnp.bfloat16)
    d_low = lax.dot_general(d_scale, cross_up, (((1,), (1,)), ((), ())), preferred_element_type=jnp.float32).astype(jnp.bfloat16)
    d_input = upstream.astype(jnp.float32) * (scale_c + 1.0) + jnp.dot(d_low, cross_down, preferred_element_type=jnp.float32)
    pooled = d_input[:, E:].astype(jnp.bfloat16)
    up_term = lax.dot_general(low_rank, d_scale, (((0,), (0,)), ((), ())), preferred_element_type=jnp.float32)
    down_term = lax.dot_general(d_low, cross_input, (((0,), (0,)), ((), ())), preferred_element_type=jnp.float32)
    return (pooled, up_term, down_term)

def adagrad_rows(rows, accum, admitted, grad):
    begin_acc = jnp.where(admitted == 1, jnp.float32(0.1), accum)
    new_acc = begin_acc + lax.optimization_barrier(jnp.mean(grad * grad, axis=1))
    new_values = rows - 0.5 * grad / (jnp.sqrt(new_acc)[:, None] + 1e-08)
    return (new_values, new_acc)

def reference(cross_input, upstream, cross_down, cross_up, cross_bias, bag_rows, bag_lengths, table_owner, table_rows, row_accum, admitted):
    block_rows = math.gcd(SAMPLES, 4096)
    block_count = SAMPLES // block_rows
    inputs = (cross_input.reshape(block_count, block_rows, F), upstream.reshape(block_count, block_rows, F))

    def step_block(running, pieces):
        pooled, up_term, down_term = cross_backward(pieces[0], pieces[1], cross_down, cross_up, cross_bias)
        return ((running[0] + up_term, running[1] + down_term), pooled)
    zeros_rf = jnp.zeros((R, F), jnp.float32)
    sums, pooled_blocks = lax.scan(step_block, (zeros_rf, zeros_rf), inputs)
    norm_scale = 1.0 / math.sqrt(SAMPLES)
    grad_up = sums[0] * norm_scale
    grad_down = sums[1] * norm_scale
    pooled = pooled_blocks.reshape(SAMPLES * NT, E).astype(jnp.float32)
    global_rows = table_owner.astype(jnp.int32)[None, :, None] * UNQ + bag_rows
    row_grad = jnp.zeros((ROWS + 1, E), jnp.float32)
    for position in range(L):
        segment = jnp.where(position < bag_lengths, global_rows[:, :, position], ROWS).reshape(-1).astype(jnp.int32)
        row_grad = row_grad + jax.ops.segment_sum(pooled, segment, num_segments=ROWS + 1)
    row_grad = row_grad[:ROWS]
    new_rows, new_accum = adagrad_rows(table_rows, row_accum, admitted, row_grad)
    return (new_rows, new_accum, grad_up, grad_down)
```

```python
import math

import jax
import jax.numpy as jnp
import numpy as np
from jax import lax
from jax.experimental import pallas as pl
from jax.experimental.pallas import tpu as pltpu
from jax.sharding import Mesh
from jax.sharding import PartitionSpec as P

NY, NZ, NX, NC = 4, 8, 4, 2
NW = NY * NZ
EMB, TABLES, RANK, UNIQ, BAG = 128, 26, 512, 512, 16
COLS = 27
XB = 7
S = 128
HALF = RANK // NC
ROWB = UNIQ // (NX * NC)
F32, BF16 = jnp.float32, jnp.bfloat16
WIDE = ("y", "z")
NARROW = ("x", "c")
ALL = WIDE + NARROW
VMEM = pl.BlockSpec(memory_space=pltpu.VMEM)
SMEM = pl.BlockSpec(memory_space=pltpu.SMEM)
SWAP = [(0, 1), (1, 0)]


def rank_order():
    order = np.arange(RANK).reshape(NW, NX, NC, 2).transpose(2, 0, 1, 3).reshape(-1)
    return np.eye(RANK, dtype=np.float32)[order]


def params():
    return pltpu.CompilerParams(vmem_limit_bytes=48 * 1024 * 1024)


def bag_kernel(core, ids_own, ids_sib, pooled_own, pooled_sib, out):
    mine = core[0]
    places = lax.broadcasted_iota(jnp.int32, (ROWB, 2 * S), 0)

    @pl.loop(0, TABLES)
    def _(t):
        ids = jnp.concatenate([ids_own[t], ids_sib[t]], axis=1)
        low = jnp.bitwise_and(ids, ROWB - 1)
        part = jnp.bitwise_and(lax.shift_right_arithmetic(ids, 6), 1)
        field = jnp.bitwise_and(lax.shift_right_arithmetic(ids, 7), 3)
        value = jnp.where(
            (ids >= 0) & (part == mine), lax.shift_left(jnp.ones_like(ids), field * 8), 0
        )
        packed = jnp.zeros((ROWB, 2 * S), jnp.int32)
        for j in range(BAG):
            packed = packed + jnp.where(places == low[j : j + 1], value[j : j + 1], 0)
        counts = jnp.concatenate(
            [
                jnp.bitwise_and(lax.shift_right_logical(packed, 8 * f), 255).astype(F32).astype(BF16)
                for f in range(NX)
            ],
            axis=0,
        )
        at = pl.multiple_of(t * EMB, EMB)
        grads = jnp.concatenate([pooled_own[:, pl.ds(at, EMB)], pooled_sib[:, pl.ds(at, EMB)]], axis=0)
        sums = jnp.dot(counts, grads, preferred_element_type=F32).astype(BF16)
        for f in range(NX):
            out[f, t] = sums[f * ROWB : (f + 1) * ROWB]


def bag_sums(core, ids_own, ids_sib, pooled_own, pooled_sib):
    return pl.pallas_call(
        bag_kernel,
        out_shape=jax.ShapeDtypeStruct((NX, TABLES, ROWB, EMB), BF16),
        in_specs=[SMEM, VMEM, VMEM, VMEM, VMEM],
        out_specs=VMEM,
        compiler_params=params(),
        name="bag_sums",
    )(core, ids_own, ids_sib, pooled_own, pooled_sib)


def dense_kernel(place, own, sib, low0, low1, low2, low3, out, wide_x, wide_low):
    me = place[0]
    lows = (low0, low1, low2, low3)
    for g in range(2):
        for k in range(NX):
            src = lax.rem(me - k + NX, NX)
            for s, ref in enumerate((own, sib)):
                at = (k * 2 + s) * S
                wide_low[g, :, at : at + S] = lows[k][s, g]
                for j in range(XB):
                    wide_x[g, at : at + S, j * EMB : (j + 1) * EMB] = ref[src, g, j]

    @pl.loop(0, XB)
    def _(j):
        cols = pl.ds(pl.multiple_of(j * EMB, EMB), EMB)
        both = []
        for g in range(2):
            part = jnp.dot(wide_low[g], wide_x[g, :, cols], preferred_element_type=F32)
            both.append(part.reshape(NW, 8, EMB))
        out[:, pl.ds(pl.multiple_of(j * 16, 16), 16), :] = jnp.concatenate(both, axis=1).astype(BF16)


def dense_sums(place, own, sib, lows):
    return pl.pallas_call(
        dense_kernel,
        out_shape=jax.ShapeDtypeStruct((NW, 16 * XB, EMB), BF16),
        in_specs=[SMEM] + [VMEM] * 6,
        out_specs=VMEM,
        scratch_shapes=[
            pltpu.VMEM((2, NX * NC * S, XB * EMB), BF16),
            pltpu.VMEM((2, HALF, NX * NC * S), BF16),
        ],
        compiler_params=params(),
        name="dense_sums",
    )(place, own, sib, *lows)


def owner_kernel(owner, got, out, total):
    total[...] = jnp.zeros_like(total)

    @pl.loop(0, TABLES)
    def _(t):
        one = got[0, t].astype(F32)
        for k in range(1, NX):
            one = one + got[k, t].astype(F32)
        to = owner[t]
        total[to] = total[to] + one

    out[...] = total[...].astype(BF16)


def owner_sums(owner, got):
    return pl.pallas_call(
        owner_kernel,
        out_shape=jax.ShapeDtypeStruct((NW, ROWB, EMB), BF16),
        in_specs=[SMEM, VMEM],
        out_specs=VMEM,
        scratch_shapes=[pltpu.VMEM((NW, ROWB, EMB), F32)],
        compiler_params=params(),
        name="owner_sums",
    )(owner, got)


def adagrad_rows(rows, accum, admitted, grad):
    begin_acc = jnp.where(admitted == 1, jnp.float32(0.1), accum)
    new_acc = begin_acc + jnp.mean(grad * grad, axis=1)
    new_values = rows - 0.5 * grad / (jnp.sqrt(new_acc)[:, None] + 1e-08)
    return (new_values, new_acc)


def local(
    cross_input,
    upstream,
    cross_down,
    cross_up,
    cross_bias,
    bag_rows,
    bag_lengths,
    table_owner,
    table_rows,
    row_accum,
    admitted,
):
    me_x, me_c = lax.axis_index("x"), lax.axis_index("c")
    position = lax.broadcasted_iota(jnp.int32, (TABLES, BAG, S), 1)
    ids = jnp.where(
        position < bag_lengths.T[:, None, :], jnp.transpose(bag_rows, (1, 2, 0)), -1
    )
    ids_sib = lax.ppermute(ids, "c", SWAP)

    d_scale = (upstream.astype(F32) * cross_input.astype(F32)).astype(BF16)

    def blocks(a):
        padded = jnp.pad(a, ((0, 0), (0, (NX * XB - COLS) * EMB)))
        return jnp.transpose(padded.reshape(S, NX, XB, EMB), (1, 2, 0, 3))

    pair = jnp.stack([blocks(d_scale), blocks(cross_input)], axis=1)
    own = lax.all_to_all(pair, "x", split_axis=0, concat_axis=0, tiled=True)
    sib = lax.ppermute(own, "c", SWAP)

    low_t = lax.dot_general(
        cross_down, cross_input, (((1,), (1,)), ((), ())), preferred_element_type=F32
    ).astype(BF16)
    d_low_t = lax.dot_general(
        cross_up, d_scale, (((1,), (1,)), ((), ())), preferred_element_type=F32
    ).astype(BF16)
    order = jnp.asarray(rank_order(), BF16)
    halves = jnp.dot(
        order, jnp.concatenate([low_t, d_low_t], axis=1), preferred_element_type=F32
    ).astype(BF16)
    halves = jnp.transpose(halves.reshape(NC, HALF, 2, S), (0, 2, 1, 3))
    keep = jnp.where(me_c == 0, halves[0], halves[1])
    give = jnp.where(me_c == 0, halves[1], halves[0])
    low0 = jnp.stack([keep, lax.ppermute(give, "c", SWAP)])
    lows = [low0] + [
        lax.ppermute(low0, "x", [(i, (i + k) % NX) for i in range(NX)]) for k in range(1, NX)
    ]

    scale_tail = lax.dot_general(
        low_t, cross_up[:, EMB:], (((0,), (0,)), ((), ())), preferred_element_type=F32
    ) + cross_bias[EMB:].astype(F32)
    tail_grad = upstream[:, EMB:].astype(F32) * (scale_tail + 1.0) + lax.dot_general(
        d_low_t, cross_down[:, EMB:], (((0,), (0,)), ((), ())), preferred_element_type=F32
    )
    pooled = tail_grad.astype(BF16)
    pooled_sib = lax.ppermute(pooled, "c", SWAP)

    core = me_c.astype(jnp.int32).reshape(1)
    sums = bag_sums(core, ids, ids_sib, pooled, pooled_sib)
    got = lax.all_to_all(sums, "x", split_axis=0, concat_axis=0, tiled=True)
    dense = dense_sums(me_x.astype(jnp.int32).reshape(1), own, sib, lows)
    rows = owner_sums(table_owner, got)

    merged = jnp.concatenate([rows, dense], axis=1)
    merged = lax.all_to_all(merged, WIDE, split_axis=0, concat_axis=0, tiled=True)
    total = jnp.sum(merged.astype(F32), axis=0)
    row_part = jnp.broadcast_to(total[:ROWB], (NX, NC, ROWB, EMB))
    dense_part = total[ROWB:].reshape(XB * 2, NX, 2, EMB)
    dense_part = jnp.transpose(dense_part, (1, 0, 2, 3)).reshape(NX, 1, XB * 4, EMB)
    dense_part = jnp.broadcast_to(dense_part, (NX, NC, XB * 4, EMB))
    final = jnp.concatenate([row_part, dense_part], axis=2).reshape(NX * NC, ROWB + XB * 4, EMB)
    final = lax.all_to_all(final, NARROW, split_axis=0, concat_axis=0, tiled=True)
    row_grad = final[:, :ROWB].reshape(UNIQ, EMB)
    new_rows, new_accum = adagrad_rows(table_rows, row_accum, admitted, row_grad)

    norm_scale = 1.0 / math.sqrt(S * NW * NX * NC)
    grads = final[:, ROWB:].reshape(NX, NC, XB, 2, 2, EMB)
    grads = jnp.where(me_c == 0, grads[:, 0], grads[:, 1])
    grads = jnp.transpose(grads, (2, 3, 0, 1, 4)).reshape(2, 2, NX * XB * EMB)
    grads = grads[:, :, : COLS * EMB] * norm_scale
    return (new_rows, new_accum, grads[0], grads[1])


def solution(mesh):
    inner = Mesh(mesh.devices.reshape(NY, NZ, NX, NC), ALL)
    return jax.shard_map(
        local,
        mesh=inner,
        in_specs=(
            P(ALL, None),
            P(ALL, None),
            P(),
            P(),
            P(),
            P(ALL, None, None),
            P(ALL, None),
            P(),
            P(WIDE, None),
            P(WIDE),
            P(WIDE),
        ),
        out_specs=(
            P(WIDE, None),
            P(WIDE),
            P(ALL, None),
            P(ALL, None),
        ),
        check_vma=False,
    )
```

```python
import math

import jax
import jax.numpy as jnp
import numpy as np
from jax import lax
from jax.experimental import pallas as pl
from jax.experimental.pallas import tpu as pltpu
from jax.sharding import Mesh
from jax.sharding import PartitionSpec as P

NY, NZ, NX, NC = 4, 8, 4, 2
NW = NY * NZ
EMB, TABLES, RANK, UNIQ, BAG = 128, 26, 512, 512, 16
COLS = 27
XB = 7
S = 128
HALF = RANK // NC
ROWB = UNIQ // (NX * NC)
PIECE = ROWB // NY
DROWS = XB * 4
MROWS = 48
F32, BF16 = jnp.float32, jnp.bfloat16
WIDE = ("y", "z")
ALL = ("y", "z", "x", "c")
VMEM = pl.BlockSpec(memory_space=pltpu.VMEM)
SMEM = pl.BlockSpec(memory_space=pltpu.SMEM)


def rank_order():
    order = np.arange(RANK).reshape(NY, NZ, NX, NC, 2).transpose(3, 2, 1, 0, 4).reshape(-1)
    return np.eye(RANK, dtype=np.float32)[order]


def params(mib=24):
    return pltpu.CompilerParams(vmem_limit_bytes=mib * 1024 * 1024)


def cost(us):
    return pl.CostEstimate(flops=int(us * 1e9), bytes_accessed=int(us * 1e5), transcendentals=0)


def pack_kernel(x, u, ids, lengths, pair, scaled, masked):
    ds = (u[...].astype(F32) * x[...].astype(F32)).astype(BF16)
    scaled[...] = ds
    for b in range(NY):
        size = min(XB, COLS - b * XB) * EMB
        cols = slice(b * XB * EMB, b * XB * EMB + size)
        pair[b, 0, :, :size] = ds[:, cols]
        pair[b, 1, :, :size] = x[:, cols]
        if size < XB * EMB:
            pair[b, :, :, size:] = jnp.zeros((2, ds.shape[0], XB * EMB - size), BF16)

    @pl.when(pl.program_id(0) == 0)
    def _():
        position = lax.broadcasted_iota(jnp.int32, (BAG, S), 0)
        for t in range(TABLES):
            masked[t] = jnp.where(position < lengths[t : t + 1], ids[t], -1)


def pack(x, u, ids, lengths):
    steps = 4
    rows = S // steps
    wide = pl.BlockSpec((rows, x.shape[1]), lambda i: (i, 0))
    every = pl.BlockSpec((TABLES, BAG, S), lambda i: (0, 0, 0))
    return pl.pallas_call(
        pack_kernel,
        grid=(steps,),
        out_shape=(
            jax.ShapeDtypeStruct((NY, 2, S, XB * EMB), BF16),
            jax.ShapeDtypeStruct(x.shape, BF16),
            jax.ShapeDtypeStruct((TABLES, BAG, S), jnp.int32),
        ),
        in_specs=[wide, wide, every, pl.BlockSpec((TABLES, S), lambda i: (0, 0))],
        out_specs=(
            pl.BlockSpec((NY, 2, rows, XB * EMB), lambda i: (0, 0, i, 0)),
            wide,
            every,
        ),
        compiler_params=params(60),
        cost_estimate=cost(1.5),
        name="pack",
    )(x, u, ids, lengths)


def halves_kernel(core, order, low, d_low, keep, give):
    for to, at in ((keep, core[0]), (give, 1 - core[0])):
        pick = order[pl.ds(pl.multiple_of(at * HALF, HALF), HALF), :]
        to[0] = jnp.dot(pick, low[...], preferred_element_type=F32).astype(BF16)
        to[1] = jnp.dot(pick, d_low[...], preferred_element_type=F32).astype(BF16)


def rank_halves(core, low, d_low):
    part = jax.ShapeDtypeStruct((2, HALF, S), BF16)
    return pl.pallas_call(
        halves_kernel,
        out_shape=(part, part),
        in_specs=[SMEM, VMEM, VMEM, VMEM],
        out_specs=(VMEM, VMEM),
        compiler_params=params(),
        cost_estimate=cost(0.5),
        name="rank_halves",
    )(core, jnp.asarray(rank_order(), BF16), low, d_low)


def bag_kernel(place, ids_own, ids_sib, pooled_own, pooled_sib, out, stage, sems):
    mine = place[3]
    places = lax.broadcasted_iota(jnp.int32, (ROWB, 2 * S), 0)

    def table(t):
        ids = jnp.concatenate([ids_own[t], ids_sib[t]], axis=1)
        low = jnp.bitwise_and(ids, ROWB - 1)
        part = jnp.bitwise_and(lax.shift_right_arithmetic(ids, 6), 1)
        field = jnp.bitwise_and(lax.shift_right_arithmetic(ids, 7), 3)
        value = jnp.where(
            (ids >= 0) & (part == mine), lax.shift_left(jnp.ones_like(ids), field * 8), 0
        )
        packed = jnp.zeros((ROWB, 2 * S), jnp.int32)
        for j in range(BAG):
            packed = packed + jnp.where(places == low[j : j + 1], value[j : j + 1], 0)
        counts = jnp.concatenate(
            [
                jnp.bitwise_and(lax.shift_right_logical(packed, 8 * f), 255).astype(F32).astype(BF16)
                for f in range(NX)
            ],
            axis=0,
        )
        at = pl.multiple_of(t * EMB, EMB)
        grads = jnp.concatenate([pooled_own[:, pl.ds(at, EMB)], pooled_sib[:, pl.ds(at, EMB)]], axis=0)
        sums = jnp.dot(counts, grads, preferred_element_type=F32).astype(BF16)
        for k in range(NX):
            for m in range(NY):
                at = (k * NY + m) * PIECE
                stage[m * NX + k, t] = sums[at : at + PIECE]

    ends = (0, 8, 16, 22, TABLES)
    copies = []
    for i in range(4):
        pl.loop(ends[i], ends[i + 1], unroll=2)(table)
        part = pl.ds(ends[i], ends[i + 1] - ends[i])
        copies.append(pltpu.make_async_copy(stage.at[:, part], out.at[:, part], sems.at[i]))
        copies[-1].start()
    for copy in copies:
        copy.wait()


def bag_sums(place, ids_own, ids_sib, pooled_own, pooled_sib):
    return pl.pallas_call(
        bag_kernel,
        out_shape=jax.ShapeDtypeStruct((NY * NX, TABLES, PIECE, EMB), BF16),
        in_specs=[SMEM, VMEM, VMEM, VMEM, VMEM],
        out_specs=pl.BlockSpec(memory_space=pl.ANY),
        scratch_shapes=[
            pltpu.VMEM((NY * NX, TABLES, PIECE, EMB), BF16),
            pltpu.SemaphoreType.DMA((4,)),
        ],
        compiler_params=params(58),
        cost_estimate=cost(1),
        name="bag_sums",
    )(place, ids_own, ids_sib, pooled_own, pooled_sib)


def gather_side(me_y, side, lows, ref, wide_x, wide_low):
    for g in range(2):
        for k in range(NY):
            src = lax.rem(me_y - k + NY, NY)
            wide_low[g, :, k * S : (k + 1) * S] = lows[k][side, g]
            wide_x[g, k * S : (k + 1) * S] = ref[src, g]


def dense_own_kernel(place, own, low0, low1, low2, low3, out, wide_x, wide_low):
    gather_side(place[1], 0, (low0, low1, low2, low3), own, wide_x, wide_low)
    for g in range(2):
        out[g] = jnp.dot(wide_low[g], wide_x[g], preferred_element_type=F32)


def dense_both_kernel(place, first, sib, low0, low1, low2, low3, out0, out1, out2, out3, wide_x, wide_low, stage):
    gather_side(place[1], 1, (low0, low1, low2, low3), sib, wide_x, wide_low)
    both = [
        first[g] + jnp.dot(wide_low[g], wide_x[g], preferred_element_type=F32) for g in range(2)
    ]
    for j in range(XB):
        pieces = [b[:, j * EMB : (j + 1) * EMB].reshape(NX, NZ, 8, EMB) for b in both]
        stage[:, :, j * 16 : (j + 1) * 16, :] = jnp.concatenate(pieces, axis=2).astype(BF16)

    for k, out in enumerate((out0, out1, out2, out3)):
        out[...] = stage[lax.rem(place[0] + k, NX)]


WIDE_SIDE = [
    pltpu.VMEM((2, NY * S, XB * EMB), BF16),
    pltpu.VMEM((2, HALF, NY * S), BF16),
]


def dense_own(place, own, lows):
    return pl.pallas_call(
        dense_own_kernel,
        out_shape=jax.ShapeDtypeStruct((2, HALF, XB * EMB), F32),
        in_specs=[SMEM] + [VMEM] * 5,
        out_specs=VMEM,
        scratch_shapes=WIDE_SIDE,
        compiler_params=params(),
        cost_estimate=cost(20),
        name="dense_own",
    )(place, own, *lows)


def dense_both(place, first, sib, lows):
    part = jax.ShapeDtypeStruct((NZ, 16 * XB, EMB), BF16)
    return pl.pallas_call(
        dense_both_kernel,
        out_shape=(part,) * NX,
        in_specs=[SMEM] + [VMEM] * 6,
        out_specs=(VMEM,) * NX,
        scratch_shapes=WIDE_SIDE + [pltpu.VMEM((NX, NZ, 16 * XB, EMB), BF16)],
        compiler_params=params(),
        cost_estimate=cost(0),
        name="dense_both",
    )(place, first, sib, *lows)


def merge_kernel(owner, got, *refs):
    parts, out, total, dense = refs[:NX], *refs[NX:]
    total[...] = jnp.zeros_like(total)

    @pl.loop(0, TABLES)
    def _(t):
        one = got[0, t].astype(F32)
        for k in range(1, NY * NX):
            one = one + got[k, t].astype(F32)
        to = owner[t]
        total[to, :PIECE] = total[to, :PIECE] + one

    add = parts[0][...].astype(F32)
    for part in parts[1:]:
        add = add + part[...].astype(F32)
    dense[...] = add
    for y in range(NY):
        for j in range(XB):
            for g in range(2):
                at, src = PIECE + j * 4 + g * 2, j * 16 + g * 8 + y * 2
                total[y * NZ : (y + 1) * NZ, at : at + 2] = dense[:, src : src + 2]
    out[...] = total[...].astype(BF16)


def merge(owner, got, parts):
    return pl.pallas_call(
        merge_kernel,
        out_shape=jax.ShapeDtypeStruct((NW, MROWS, EMB), BF16),
        in_specs=[SMEM] + [VMEM] * (1 + NX),
        out_specs=VMEM,
        scratch_shapes=[
            pltpu.VMEM((NW, MROWS, EMB), F32),
            pltpu.VMEM((NZ, 16 * XB, EMB), F32),
        ],
        compiler_params=params(),
        cost_estimate=cost(0),
        name="merge",
    )(owner, got, *parts)


def split_kernel(got, rows, up, down, stage):
    for y in range(NY):
        one = got[y * NZ].astype(F32)
        for z in range(1, NZ):
            one = one + got[y * NZ + z].astype(F32)
        for n in range(NX * NC):
            rows[n, y * PIECE : (y + 1) * PIECE] = one[:PIECE]
        stage[y] = one[PIECE:] * (1.0 / math.sqrt(S * NW * NX * NC))
    for y in range(NY):
        for j in range(XB):
            at = (y * XB + j) * EMB
            if at < COLS * EMB:
                for g, to in enumerate((up, down)):
                    to[:, at : at + EMB] = stage[y, j * 4 + g * 2 : j * 4 + g * 2 + 2]


def split(got):
    grad = jax.ShapeDtypeStruct((2, COLS * EMB), F32)
    return pl.pallas_call(
        split_kernel,
        out_shape=(jax.ShapeDtypeStruct((NX * NC, ROWB, EMB), F32), grad, grad),
        in_specs=[VMEM],
        out_specs=(VMEM, VMEM, VMEM),
        scratch_shapes=[pltpu.VMEM((NY, MROWS - PIECE, EMB), F32)],
        compiler_params=params(),
        cost_estimate=cost(0),
        name="split",
    )(got)


def adagrad_rows(rows, accum, admitted, grad):
    begin_acc = jnp.where(admitted == 1, jnp.float32(0.1), accum)
    new_acc = begin_acc + jnp.mean(grad * grad, axis=1)
    new_values = rows - 0.5 * grad / (jnp.sqrt(new_acc)[:, None] + 1e-08)
    return (new_values, new_acc)


def local(
    cross_input,
    upstream,
    cross_down,
    cross_up,
    cross_bias,
    bag_rows,
    bag_lengths,
    table_owner,
    table_rows,
    row_accum,
    admitted,
):
    me_y, me_z, me_x, me_c = (lax.axis_index(a).astype(jnp.int32) for a in ALL)
    core, place = me_c.reshape(1), jnp.stack([me_x, me_y, me_z, me_c])

    def send(a, axis, k):
        size = lax.axis_size(axis)
        return lax.ppermute(a, axis, [(i, (i + k) % size) for i in range(size)])

    pair, d_scale, ids = pack(
        cross_input, upstream, jnp.transpose(bag_rows, (1, 2, 0)), bag_lengths.T
    )
    own = lax.all_to_all(pair, "y", split_axis=0, concat_axis=0, tiled=True)
    ids_sib = send(ids, "c", 1)

    low_t = lax.dot_general(
        cross_down, cross_input, (((1,), (1,)), ((), ())), preferred_element_type=F32
    ).astype(BF16)
    d_low_t = lax.dot_general(
        cross_up, d_scale, (((1,), (1,)), ((), ())), preferred_element_type=F32
    ).astype(BF16)
    scale_tail = lax.dot_general(
        low_t, cross_up[:, EMB:], (((0,), (0,)), ((), ())), preferred_element_type=F32
    ) + cross_bias[EMB:].astype(F32)
    tail_grad = upstream[:, EMB:].astype(F32) * (scale_tail + 1.0) + lax.dot_general(
        d_low_t, cross_down[:, EMB:], (((0,), (0,)), ((), ())), preferred_element_type=F32
    )
    pooled = tail_grad.astype(BF16)
    pooled_sib = send(pooled, "c", 1)

    keep, give = rank_halves(core, low_t, d_low_t)
    low0 = jnp.stack([keep, send(give, "c", 1)])
    low0, pooled_sib = lax.optimization_barrier((low0, pooled_sib))
    lows = [low0] + [send(low0, "y", k) for k in range(1, NY)]

    sums = bag_sums(place, ids, ids_sib, pooled, pooled_sib)
    own, sums = lax.optimization_barrier((own, sums))
    sib = send(own, "c", 1)
    got = lax.all_to_all(sums, ("y", "x"), split_axis=0, concat_axis=0, tiled=True)
    parts = dense_both(place, dense_own(place, own, lows), sib, lows)
    parts = [parts[0]] + [send(parts[k], "x", k) for k in range(1, NX)]
    merged = merge(table_owner, got, parts)
    merged = lax.all_to_all(merged, WIDE, split_axis=0, concat_axis=0, tiled=True)
    rows, grad_up, grad_down = split(merged)
    rows = lax.all_to_all(rows, ("x", "c"), split_axis=0, concat_axis=0, tiled=True)
    new_rows, new_accum = adagrad_rows(
        table_rows, row_accum, admitted, rows.reshape(UNIQ, EMB)
    )
    return (new_rows, new_accum, grad_up, grad_down)


def solution(mesh):
    inner = Mesh(mesh.devices.reshape(NY, NZ, NX, NC), ALL)
    return jax.shard_map(
        local,
        mesh=inner,
        in_specs=(
            P(ALL, None),
            P(ALL, None),
            P(),
            P(),
            P(),
            P(ALL, None, None),
            P(ALL, None),
            P(),
            P(WIDE, None),
            P(WIDE),
            P(WIDE),
        ),
        out_specs=(
            P(WIDE, None),
            P(WIDE),
            P(ALL, None),
            P(ALL, None),
        ),
        check_vma=False,
    )
```

```python
import math

import jax
import jax.numpy as jnp
import numpy as np
from jax import lax
from jax.experimental import pallas as pl
from jax.experimental.pallas import tpu as pltpu
from jax.sharding import Mesh
from jax.sharding import PartitionSpec as P

NY, NZ, NX, NC = 4, 8, 4, 2
NW = NY * NZ
EMB, TABLES, RANK, UNIQ, BAG = 128, 26, 512, 512, 16
COLS = 27
XB = 7
S = 128
HALF = RANK // NC
ROWB = UNIQ // (NX * NC)
PIECE = ROWB // NY
DROWS = XB * 4
MROWS = 48
TX = 7
NONE = 256.0
F32, BF16 = jnp.float32, jnp.bfloat16
WIDE = ("y", "z")
ALL = ("y", "z", "x", "c")
VMEM = pl.BlockSpec(memory_space=pltpu.VMEM)
SMEM = pl.BlockSpec(memory_space=pltpu.SMEM)


def rank_order():
    order = np.arange(RANK).reshape(NW, NX, NC, 2).transpose(2, 1, 3, 0).reshape(-1)
    return np.eye(RANK, dtype=np.float32)[order]


def params(mib=24):
    return pltpu.CompilerParams(vmem_limit_bytes=mib * 1024 * 1024)


def cost(us):
    return pl.CostEstimate(flops=int(us * 1e9), bytes_accessed=int(us * 1e5), transcendentals=0)


def axis(name):
    return lax.axis_index(name).astype(jnp.int32)


def pack_kernel(x, u, ids, lengths, pair, coded):
    ds = (u[...].astype(F32) * x[...].astype(F32)).astype(BF16)
    for b in range(NY):
        size = min(XB, COLS - b * XB) * EMB
        cols = slice(b * XB * EMB, b * XB * EMB + size)
        pair[b, 0, :, :size] = ds[:, cols]
        pair[b, 1, :, :size] = x[:, cols]
        if size < XB * EMB:
            pair[b, :, :, size:] = jnp.zeros((2, ds.shape[0], XB * EMB - size), BF16)

    @pl.when(pl.program_id(0) == 0)
    def _():
        position = lax.broadcasted_iota(jnp.int32, (BAG, S), 0)
        for t in range(TABLES):
            code = jnp.where(position < lengths[t : t + 1], (ids[t] - 256).astype(F32), NONE)
            coded[t] = code.astype(BF16)


def pack(x, u, ids, lengths):
    steps = 4
    rows = S // steps
    wide = pl.BlockSpec((rows, x.shape[1]), lambda i: (i, 0))
    every = pl.BlockSpec((TABLES, BAG, S), lambda i: (0, 0, 0))
    return pl.pallas_call(
        pack_kernel,
        grid=(steps,),
        out_shape=(
            jax.ShapeDtypeStruct((NY, 2, S, XB * EMB), BF16),
            jax.ShapeDtypeStruct((TABLES, BAG, S), BF16),
        ),
        in_specs=[wide, wide, every, pl.BlockSpec((TABLES, S), lambda i: (0, 0))],
        out_specs=(
            pl.BlockSpec((NY, 2, rows, XB * EMB), lambda i: (0, 0, i, 0)),
            every,
        ),
        compiler_params=params(60),
        cost_estimate=cost(1.5),
        name="pack",
    )(x, u, ids, lengths)


def cross_kernel(
    x_in, u_in, down_in, up_in, bias, order, coded, keep, give, out0, out1, out2, out3, x, u, down, up, pooled, sems
):
    spans = [(at, min(at + XB * EMB, COLS * EMB)) for at in range(0, COLS * EMB, XB * EMB)]
    first = [pltpu.make_async_copy(x_in, x, sems.at[0]), pltpu.make_async_copy(u_in, u, sems.at[1])]
    loads = []
    for w, (src, to) in enumerate(((down_in, down), (up_in, up))):
        loads.append([])
        for i, (begin, end) in enumerate(spans):
            at = pl.ds(begin, end - begin)
            loads[w].append(
                pltpu.make_async_copy(src.at[:, at], to.at[:, at], sems.at[2 + w * NY + i])
            )
    for copy in first[:1] + loads[0] + first[1:] + loads[1]:
        copy.start()

    def low_of(weight, copies, piece):
        total = jnp.zeros((RANK, S), F32)
        for copy, (begin, end) in zip(copies, spans):
            copy.wait()
            total = total + lax.dot_general(
                weight[:, begin:end], piece(begin, end), (((1,), (1,)), ((), ())), preferred_element_type=F32
            )
        return total.astype(BF16)

    first[0].wait()
    low = low_of(down, loads[0], lambda begin, end: x[:, begin:end])
    first[1].wait()
    d_low = low_of(
        up,
        loads[1],
        lambda begin, end: (u[:, begin:end].astype(F32) * x[:, begin:end].astype(F32)).astype(BF16),
    )
    for to, at in ((keep, axis("c")), (give, 1 - axis("c"))):
        pick = order[pl.ds(pl.multiple_of(at * HALF, HALF), HALF), :]
        for g, one in enumerate((low, d_low)):
            to[g] = jnp.dot(pick, one, preferred_element_type=F32).astype(BF16)
    low, d_low = low.T, d_low.T
    size = 2 * 256
    for at in range(EMB, COLS * EMB, size):
        cols = slice(at, min(at + size, COLS * EMB))
        scale = jnp.dot(low, up[:, cols], preferred_element_type=F32) + bias[cols].astype(F32)[None, :]
        back = jnp.dot(d_low, down[:, cols], preferred_element_type=F32)
        grad = u[:, cols].astype(F32) * (scale + 1.0) + back
        pooled[:, cols.start - EMB : cols.stop - EMB] = grad.astype(BF16)
    for k, out in enumerate((out0, out1, out2, out3)):
        to = lax.rem(axis("x") + k, NX)
        for i in range(TX):

            def put(out=out, to=to, i=i):
                t = to * TX + i
                out[i, :S] = pooled[:, pl.ds(pl.multiple_of(t * EMB, EMB), EMB)]
                out[i, S:] = coded[t]

            def blank(out=out, i=i):
                out[i, :S] = jnp.zeros((S, EMB), BF16)
                out[i, S:] = jnp.full((BAG, S), NONE, BF16)

            if (NX - 1) * TX + i < TABLES:
                put()
            else:
                pl.when(to < NX - 1)(put)
                pl.when(to == NX - 1)(blank)


def cross(x, u, down, up, bias, coded):
    half = jax.ShapeDtypeStruct((2, HALF, S), BF16)
    part = jax.ShapeDtypeStruct((TX, S + BAG, EMB), BF16)
    anywhere = pl.BlockSpec(memory_space=pl.ANY)
    return pl.pallas_call(
        cross_kernel,
        out_shape=(half, half) + (part,) * NX,
        in_specs=[anywhere] * 4 + [VMEM] * 3,
        out_specs=(VMEM,) * (2 + NX),
        scratch_shapes=[
            pltpu.VMEM(x.shape, BF16),
            pltpu.VMEM(x.shape, BF16),
            pltpu.VMEM(down.shape, BF16),
            pltpu.VMEM(down.shape, BF16),
            pltpu.VMEM((S, TABLES * EMB), BF16),
            pltpu.SemaphoreType.DMA((2 + 2 * NY,)),
        ],
        compiler_params=params(54),
        cost_estimate=cost(5),
        name="cross",
    )(x, u, down, up, bias, jnp.asarray(rank_order(), BF16), coded)


def bag_kernel(block0, block1, block2, block3, keep, give):
    blocks = (block0, block1, block2, block3)
    places = lax.broadcasted_iota(jnp.int32, (ROWB, NX * S), 0)

    @pl.loop(0, TX)
    def _(i):
        ids = jnp.concatenate([b[i, S:].astype(F32) for b in blocks], axis=1).astype(jnp.int32) + 256
        low = jnp.bitwise_and(ids, ROWB - 1)
        part = jnp.bitwise_and(lax.shift_right_arithmetic(ids, 6), 1)
        field = jnp.bitwise_and(lax.shift_right_arithmetic(ids, 7), 3)
        value = jnp.where(ids < UNIQ, lax.shift_left(jnp.ones_like(ids), field * 8), 0)
        grads = jnp.concatenate([b[i, :S] for b in blocks], axis=0)
        for out, mine in ((keep, axis("c")), (give, 1 - axis("c"))):
            worth = jnp.where(part == mine, value, 0)
            packed = jnp.zeros((ROWB, NX * S), jnp.int32)
            for j in range(BAG):
                packed = packed + jnp.where(places == low[j : j + 1], worth[j : j + 1], 0)
            counts = jnp.concatenate(
                [
                    jnp.bitwise_and(lax.shift_right_logical(packed, 8 * f), 255)
                    .astype(F32)
                    .astype(BF16)
                    for f in range(NX)
                ],
                axis=0,
            )
            out[i] = jnp.dot(counts, grads, preferred_element_type=F32).astype(out.dtype)


def bag_sums(blocks):
    shape = (TX, NX * ROWB, EMB)
    return pl.pallas_call(
        bag_kernel,
        out_shape=(jax.ShapeDtypeStruct(shape, F32), jax.ShapeDtypeStruct(shape, BF16)),
        in_specs=[VMEM] * NX,
        out_specs=(VMEM, VMEM),
        compiler_params=params(),
        cost_estimate=cost(10),
        name="bag_sums",
    )(*blocks)


def bag_add_kernel(keep, got, dense, out):
    sums = (keep[...] + got[...].astype(F32)).astype(BF16)
    for k in range(NX):
        for m in range(NY):
            at = (k * NY + m) * PIECE
            for i in range(TX):
                out[m * NX + k, i * PIECE : (i + 1) * PIECE] = sums[i, at : at + PIECE]
    out[:, TX * PIECE :] = dense[...]


def bag_add(keep, got, dense):
    return pl.pallas_call(
        bag_add_kernel,
        out_shape=jax.ShapeDtypeStruct((NY * NX, TX * PIECE + XB * NW, EMB), BF16),
        in_specs=[VMEM] * 3,
        out_specs=VMEM,
        compiler_params=params(),
        cost_estimate=cost(0),
        name="bag_add",
    )(keep, got, dense)


def gather_side(me_y, side, lows, ref, wide_x, wide_low):
    for g in range(2):
        for k in range(NY):
            src = lax.rem(me_y - k + NY, NY)
            wide_low[g, :, k * S : (k + 1) * S] = lows[k][side, g]
            wide_x[g, k * S : (k + 1) * S] = ref[src, g]


def dense_own_kernel(own, low0, low1, low2, low3, out, wide_x, wide_low):
    gather_side(axis("y"), 0, (low0, low1, low2, low3), own, wide_x, wide_low)
    for g in range(2):
        out[g] = jnp.dot(wide_low[g], wide_x[g], preferred_element_type=F32)


def dense_both_kernel(first, sib, low0, low1, low2, low3, out, wide_x, wide_low):
    gather_side(axis("y"), 1, (low0, low1, low2, low3), sib, wide_x, wide_low)
    for g in range(2):
        sums = first[g] + jnp.dot(wide_low[g], wide_x[g], preferred_element_type=F32)
        sums = sums.astype(BF16)
        for x in range(NX):
            for p in range(2):
                at = (x * 2 + p) * NW
                for j in range(XB):
                    out[(g * 2 + p) * NX + x, j * NW : (j + 1) * NW] = sums[
                        at : at + NW, j * EMB : (j + 1) * EMB
                    ]


WIDE_SIDE = [
    pltpu.VMEM((2, NY * S, XB * EMB), BF16),
    pltpu.VMEM((2, HALF, NY * S), BF16),
]


def dense_own(own, lows):
    return pl.pallas_call(
        dense_own_kernel,
        out_shape=jax.ShapeDtypeStruct((2, HALF, XB * EMB), F32),
        in_specs=[VMEM] * 5,
        out_specs=VMEM,
        scratch_shapes=WIDE_SIDE,
        compiler_params=params(),
        cost_estimate=cost(10),
        name="dense_own",
    )(own, *lows)


def dense_both(first, sib, lows):
    return pl.pallas_call(
        dense_both_kernel,
        out_shape=jax.ShapeDtypeStruct((NY * NX, XB * NW, EMB), BF16),
        in_specs=[VMEM] * 6,
        out_specs=VMEM,
        scratch_shapes=WIDE_SIDE,
        compiler_params=params(),
        cost_estimate=cost(0),
        name="dense_both",
    )(first, sib, *lows)


def merge_kernel(owner, got, out, total):
    total[...] = jnp.zeros_like(total)
    for t in range(TABLES):
        x, i = t // TX, t % TX
        one = got[x, i * PIECE : (i + 1) * PIECE].astype(F32)
        for y in range(1, NY):
            one = one + got[y * NX + x, i * PIECE : (i + 1) * PIECE].astype(F32)
        to = owner[t]
        total[to, :PIECE] = total[to, :PIECE] + one
    for y in range(NY):
        for j in range(XB):
            at = TX * PIECE + j * NW
            one = got[y * NX, at : at + NW].astype(F32)
            for x in range(1, NX):
                one = one + got[y * NX + x, at : at + NW].astype(F32)
            total[:, PIECE + y * XB + j, :] = one
    out[...] = total[...].astype(BF16)


def merge(owner, got):
    return pl.pallas_call(
        merge_kernel,
        out_shape=jax.ShapeDtypeStruct((NW, MROWS, EMB), BF16),
        in_specs=[SMEM, VMEM],
        out_specs=VMEM,
        scratch_shapes=[pltpu.VMEM((NW, MROWS, EMB), F32)],
        compiler_params=params(),
        cost_estimate=cost(0),
        name="merge",
    )(owner, got)


def split_kernel(got, rows, up, down, stage):
    for y in range(NY):
        one = got[y * NZ].astype(F32)
        for z in range(1, NZ):
            one = one + got[y * NZ + z].astype(F32)
        for n in range(NX * NC):
            rows[n, y * PIECE : (y + 1) * PIECE] = one[:PIECE]
        stage[y] = one[PIECE:] * (1.0 / math.sqrt(S * NW * NX * NC))
    for y in range(NY):
        for j in range(XB):
            at = (y * XB + j) * EMB
            if at < COLS * EMB:
                for g, to in enumerate((up, down)):
                    for p in range(2):
                        to[p : p + 1, at : at + EMB] = stage[g * 2 + p, y * XB + j : y * XB + j + 1]


def split(got):
    grad = jax.ShapeDtypeStruct((2, COLS * EMB), F32)
    return pl.pallas_call(
        split_kernel,
        out_shape=(jax.ShapeDtypeStruct((NX * NC, ROWB, EMB), F32), grad, grad),
        in_specs=[VMEM],
        out_specs=(VMEM, VMEM, VMEM),
        scratch_shapes=[pltpu.VMEM((NY, MROWS - PIECE, EMB), F32)],
        compiler_params=params(),
        cost_estimate=cost(0),
        name="split",
    )(got)


def adagrad_rows(rows, accum, admitted, grad):
    begin_acc = jnp.where(admitted == 1, jnp.float32(0.1), accum)
    new_acc = begin_acc + jnp.mean(grad * grad, axis=1)
    new_values = rows - 0.5 * grad / (jnp.sqrt(new_acc)[:, None] + 1e-08)
    return (new_values, new_acc)


def local(
    cross_input,
    upstream,
    cross_down,
    cross_up,
    cross_bias,
    bag_rows,
    bag_lengths,
    table_owner,
    table_rows,
    row_accum,
    admitted,
):
    def send(a, axis, k):
        size = lax.axis_size(axis)
        return lax.ppermute(a, axis, [(i, (i + k) % size) for i in range(size)])

    pair, coded = pack(
        cross_input, upstream, jnp.transpose(bag_rows, (1, 2, 0)), bag_lengths.T
    )
    own = lax.all_to_all(pair, "y", split_axis=0, concat_axis=0, tiled=True)
    keep, give, *blocks = cross(
        cross_input, upstream, cross_down, cross_up, cross_bias, coded
    )
    low0 = jnp.stack([keep, send(give, "c", 1)])
    lows = [low0] + [send(low0, "y", k) for k in range(1, NY)]

    blocks = [blocks[0]] + [send(blocks[k], "x", k) for k in range(1, NX)]
    keep, give = bag_sums(blocks)
    sib = send(own, "c", 1)
    dense = dense_both(dense_own(own, lows), sib, lows)
    got = send(give, "c", 1)
    got, dense = lax.optimization_barrier((got, dense))
    sums = bag_add(keep, got, dense)
    got = lax.all_to_all(sums, ("y", "x"), split_axis=0, concat_axis=0, tiled=True)
    merged = merge(table_owner, got)
    merged = lax.all_to_all(merged, WIDE, split_axis=0, concat_axis=0, tiled=True)
    rows, grad_up, grad_down = split(merged)
    rows = lax.all_to_all(rows, ("x", "c"), split_axis=0, concat_axis=0, tiled=True)
    new_rows, new_accum = adagrad_rows(
        table_rows, row_accum, admitted, rows.reshape(UNIQ, EMB)
    )
    return (new_rows, new_accum, grad_up, grad_down)


def solution(mesh):
    inner = Mesh(mesh.devices.reshape(NY, NZ, NX, NC), ALL)
    return jax.shard_map(
        local,
        mesh=inner,
        in_specs=(
            P(ALL, None),
            P(ALL, None),
            P(),
            P(),
            P(),
            P(ALL, None, None),
            P(ALL, None),
            P(),
            P(WIDE, None),
            P(WIDE),
            P(WIDE),
        ),
        out_specs=(
            P(WIDE, None),
            P(WIDE),
            P(ALL, None),
            P(ALL, None),
        ),
        check_vma=False,
    )
```

```python
import math

import jax
import jax.numpy as jnp
import numpy as np
from jax import lax
from jax.experimental import pallas as pl
from jax.experimental.pallas import tpu as pltpu
from jax.sharding import Mesh
from jax.sharding import PartitionSpec as P

NY, NZ, NX, NC = 4, 8, 4, 2
NW = NY * NZ
EMB, TABLES, RANK, UNIQ, BAG = 128, 26, 512, 512, 16
COLS = 27
XB = 7
S = 128
HALF = RANK // NC
ROWB = UNIQ // (NX * NC)
PIECE = ROWB // NY
DROWS = XB * 4
MROWS = 48
TX = 7
NONE = 256.0
F32, BF16 = jnp.float32, jnp.bfloat16
WIDE = ("y", "z")
ALL = ("y", "z", "x", "c")
VMEM = pl.BlockSpec(memory_space=pltpu.VMEM)
SMEM = pl.BlockSpec(memory_space=pltpu.SMEM)


def rank_order():
    order = np.arange(RANK).reshape(NY, NZ, NX, NC, 2).transpose(3, 2, 1, 0, 4).reshape(-1)
    return np.eye(RANK, dtype=np.float32)[order]


def params(mib=24):
    return pltpu.CompilerParams(vmem_limit_bytes=mib * 1024 * 1024)


def cost(us):
    return pl.CostEstimate(flops=int(us * 1e9), bytes_accessed=int(us * 1e5), transcendentals=0)


def axis(name):
    return lax.axis_index(name).astype(jnp.int32)


def pack_kernel(x, u, ids, lengths, pair, coded):
    ds = (u[...].astype(F32) * x[...].astype(F32)).astype(BF16)
    for b in range(NY):
        size = min(XB, COLS - b * XB) * EMB
        cols = slice(b * XB * EMB, b * XB * EMB + size)
        pair[b, 0, :, :size] = ds[:, cols]
        pair[b, 1, :, :size] = x[:, cols]
        if size < XB * EMB:
            pair[b, :, :, size:] = jnp.zeros((2, ds.shape[0], XB * EMB - size), BF16)

    @pl.when(pl.program_id(0) == 0)
    def _():
        position = lax.broadcasted_iota(jnp.int32, (BAG, S), 0)
        for t in range(TABLES):
            code = jnp.where(position < lengths[t : t + 1], (ids[t] - 256).astype(F32), NONE)
            coded[t] = code.astype(BF16)


def pack(x, u, ids, lengths):
    steps = 4
    rows = S // steps
    wide = pl.BlockSpec((rows, x.shape[1]), lambda i: (i, 0))
    every = pl.BlockSpec((TABLES, BAG, S), lambda i: (0, 0, 0))
    return pl.pallas_call(
        pack_kernel,
        grid=(steps,),
        out_shape=(
            jax.ShapeDtypeStruct((NY, 2, S, XB * EMB), BF16),
            jax.ShapeDtypeStruct((TABLES, BAG, S), BF16),
        ),
        in_specs=[wide, wide, every, pl.BlockSpec((TABLES, S), lambda i: (0, 0))],
        out_specs=(
            pl.BlockSpec((NY, 2, rows, XB * EMB), lambda i: (0, 0, i, 0)),
            every,
        ),
        compiler_params=params(60),
        cost_estimate=cost(1.5),
        name="pack",
    )(x, u, ids, lengths)


def cross_kernel(
    x_in, u_in, down_in, up_in, bias, order, coded, keep, give, out0, out1, out2, out3, x, u, down, up, pooled, sems
):
    spans = [(at, min(at + XB * EMB, COLS * EMB)) for at in range(0, COLS * EMB, XB * EMB)]
    first = [pltpu.make_async_copy(x_in, x, sems.at[0]), pltpu.make_async_copy(u_in, u, sems.at[1])]
    loads = []
    for w, (src, to) in enumerate(((down_in, down), (up_in, up))):
        loads.append([])
        for i, (begin, end) in enumerate(spans):
            at = pl.ds(begin, end - begin)
            loads[w].append(
                pltpu.make_async_copy(src.at[:, at], to.at[:, at], sems.at[2 + w * NY + i])
            )
    for copy in first[:1] + loads[0] + first[1:] + loads[1]:
        copy.start()

    def low_of(weight, copies, piece):
        total = jnp.zeros((RANK, S), F32)
        for copy, (begin, end) in zip(copies, spans):
            copy.wait()
            total = total + lax.dot_general(
                weight[:, begin:end], piece(begin, end), (((1,), (1,)), ((), ())), preferred_element_type=F32
            )
        return total.astype(BF16)

    first[0].wait()
    low = low_of(down, loads[0], lambda begin, end: x[:, begin:end])
    first[1].wait()
    d_low = low_of(
        up,
        loads[1],
        lambda begin, end: (u[:, begin:end].astype(F32) * x[:, begin:end].astype(F32)).astype(BF16),
    )
    for to, at in ((keep, axis("c")), (give, 1 - axis("c"))):
        pick = order[pl.ds(pl.multiple_of(at * HALF, HALF), HALF), :]
        for g, one in enumerate((low, d_low)):
            to[g] = jnp.dot(pick, one, preferred_element_type=F32).astype(BF16)
    low, d_low = low.T, d_low.T
    size = 2 * 256
    for at in range(EMB, COLS * EMB, size):
        cols = slice(at, min(at + size, COLS * EMB))
        scale = jnp.dot(low, up[:, cols], preferred_element_type=F32) + bias[cols].astype(F32)[None, :]
        back = jnp.dot(d_low, down[:, cols], preferred_element_type=F32)
        grad = u[:, cols].astype(F32) * (scale + 1.0) + back
        pooled[:, cols.start - EMB : cols.stop - EMB] = grad.astype(BF16)
    for k, out in enumerate((out0, out1, out2, out3)):
        to = lax.rem(axis("x") + k, NX)
        for i in range(TX):

            def put(out=out, to=to, i=i):
                t = to * TX + i
                out[i, :S] = pooled[:, pl.ds(pl.multiple_of(t * EMB, EMB), EMB)]
                out[i, S:] = coded[t]

            def blank(out=out, i=i):
                out[i, :S] = jnp.zeros((S, EMB), BF16)
                out[i, S:] = jnp.full((BAG, S), NONE, BF16)

            if (NX - 1) * TX + i < TABLES:
                put()
            else:
                pl.when(to < NX - 1)(put)
                pl.when(to == NX - 1)(blank)


def cross(x, u, down, up, bias, coded):
    half = jax.ShapeDtypeStruct((2, HALF, S), BF16)
    part = jax.ShapeDtypeStruct((TX, S + BAG, EMB), BF16)
    anywhere = pl.BlockSpec(memory_space=pl.ANY)
    return pl.pallas_call(
        cross_kernel,
        out_shape=(half, half) + (part,) * NX,
        in_specs=[anywhere] * 4 + [VMEM] * 3,
        out_specs=(VMEM,) * (2 + NX),
        scratch_shapes=[
            pltpu.VMEM(x.shape, BF16),
            pltpu.VMEM(x.shape, BF16),
            pltpu.VMEM(down.shape, BF16),
            pltpu.VMEM(down.shape, BF16),
            pltpu.VMEM((S, TABLES * EMB), BF16),
            pltpu.SemaphoreType.DMA((2 + 2 * NY,)),
        ],
        compiler_params=params(54),
        cost_estimate=cost(5),
        name="cross",
    )(x, u, down, up, bias, jnp.asarray(rank_order(), BF16), coded)


def bag_kernel(block0, block1, block2, block3, keep, give):
    blocks = (block0, block1, block2, block3)
    places = lax.broadcasted_iota(jnp.int32, (ROWB, NX * S), 0)

    @pl.loop(0, TX)
    def _(i):
        ids = jnp.concatenate([b[i, S:].astype(F32) for b in blocks], axis=1).astype(jnp.int32) + 256
        low = jnp.bitwise_and(ids, ROWB - 1)
        part = jnp.bitwise_and(lax.shift_right_arithmetic(ids, 6), 1)
        field = jnp.bitwise_and(lax.shift_right_arithmetic(ids, 7), 3)
        value = jnp.where(ids < UNIQ, lax.shift_left(jnp.ones_like(ids), field * 8), 0)
        grads = jnp.concatenate([b[i, :S] for b in blocks], axis=0)
        for out, mine in ((keep, axis("c")), (give, 1 - axis("c"))):
            worth = jnp.where(part == mine, value, 0)
            packed = jnp.zeros((ROWB, NX * S), jnp.int32)
            for j in range(BAG):
                packed = packed + jnp.where(places == low[j : j + 1], worth[j : j + 1], 0)
            counts = jnp.concatenate(
                [
                    jnp.bitwise_and(lax.shift_right_logical(packed, 8 * f), 255)
                    .astype(F32)
                    .astype(BF16)
                    for f in range(NX)
                ],
                axis=0,
            )
            out[i] = jnp.dot(counts, grads, preferred_element_type=F32).astype(out.dtype)


def bag_sums(blocks):
    shape = (TX, NX * ROWB, EMB)
    return pl.pallas_call(
        bag_kernel,
        out_shape=(jax.ShapeDtypeStruct(shape, F32), jax.ShapeDtypeStruct(shape, BF16)),
        in_specs=[VMEM] * NX,
        out_specs=(VMEM, VMEM),
        compiler_params=params(),
        cost_estimate=cost(10),
        name="bag_sums",
    )(*blocks)


def bag_add_kernel(keep, got, out):
    sums = (keep[...] + got[...].astype(F32)).astype(BF16)
    for k in range(NX):
        for m in range(NY):
            at = (k * NY + m) * PIECE
            out[m * NX + k] = sums[:, at : at + PIECE]


def bag_add(keep, got):
    return pl.pallas_call(
        bag_add_kernel,
        out_shape=jax.ShapeDtypeStruct((NY * NX, TX, PIECE, EMB), BF16),
        in_specs=[VMEM, VMEM],
        out_specs=VMEM,
        compiler_params=params(),
        cost_estimate=cost(0),
        name="bag_add",
    )(keep, got)


def gather_side(me_y, side, lows, ref, wide_x, wide_low):
    for g in range(2):
        for k in range(NY):
            src = lax.rem(me_y - k + NY, NY)
            wide_low[g, :, k * S : (k + 1) * S] = lows[k][side, g]
            wide_x[g, k * S : (k + 1) * S] = ref[src, g]


def dense_own_kernel(own, low0, low1, low2, low3, out, wide_x, wide_low):
    gather_side(axis("y"), 0, (low0, low1, low2, low3), own, wide_x, wide_low)
    for g in range(2):
        out[g] = jnp.dot(wide_low[g], wide_x[g], preferred_element_type=F32)


def dense_both_kernel(first, sib, low0, low1, low2, low3, out0, out1, out2, out3, wide_x, wide_low, stage):
    gather_side(axis("y"), 1, (low0, low1, low2, low3), sib, wide_x, wide_low)
    both = [
        first[g] + jnp.dot(wide_low[g], wide_x[g], preferred_element_type=F32) for g in range(2)
    ]
    for j in range(XB):
        pieces = [b[:, j * EMB : (j + 1) * EMB].reshape(NX, NZ, 8, EMB) for b in both]
        stage[:, :, j * 16 : (j + 1) * 16, :] = jnp.concatenate(pieces, axis=2).astype(BF16)

    for k, out in enumerate((out0, out1, out2, out3)):
        out[...] = stage[lax.rem(axis("x") + k, NX)]


WIDE_SIDE = [
    pltpu.VMEM((2, NY * S, XB * EMB), BF16),
    pltpu.VMEM((2, HALF, NY * S), BF16),
]


def dense_own(own, lows):
    return pl.pallas_call(
        dense_own_kernel,
        out_shape=jax.ShapeDtypeStruct((2, HALF, XB * EMB), F32),
        in_specs=[VMEM] * 5,
        out_specs=VMEM,
        scratch_shapes=WIDE_SIDE,
        compiler_params=params(),
        cost_estimate=cost(10),
        name="dense_own",
    )(own, *lows)


def dense_both(first, sib, lows):
    part = jax.ShapeDtypeStruct((NZ, 16 * XB, EMB), BF16)
    return pl.pallas_call(
        dense_both_kernel,
        out_shape=(part,) * NX,
        in_specs=[VMEM] * 6,
        out_specs=(VMEM,) * NX,
        scratch_shapes=WIDE_SIDE + [pltpu.VMEM((NX, NZ, 16 * XB, EMB), BF16)],
        compiler_params=params(),
        cost_estimate=cost(0),
        name="dense_both",
    )(first, sib, *lows)


def across_kernel(part0, part1, part2, part3, out):
    total = part0[...].astype(F32) + part1[...].astype(F32)
    out[...] = total + (part2[...].astype(F32) + part3[...].astype(F32))


def across(parts):
    return pl.pallas_call(
        across_kernel,
        out_shape=jax.ShapeDtypeStruct((NZ, 16 * XB, EMB), F32),
        in_specs=[VMEM] * NX,
        out_specs=VMEM,
        compiler_params=params(),
        cost_estimate=cost(10),
        name="across",
    )(*parts)


def merge_kernel(owner, got, dense, *refs):
    out, total = refs
    total[...] = jnp.zeros_like(total)

    for t in range(TABLES):
        x, i = t // TX, t % TX
        one = got[x, i].astype(F32)
        for y in range(1, NY):
            one = one + got[y * NX + x, i].astype(F32)
        to = owner[t]
        total[to, :PIECE] = total[to, :PIECE] + one

    for y in range(NY):
        for j in range(XB):
            for g in range(2):
                at, src = PIECE + j * 4 + g * 2, j * 16 + g * 8 + y * 2
                total[y * NZ : (y + 1) * NZ, at : at + 2] = dense[:, src : src + 2]
    out[...] = total[...].astype(BF16)


def merge(owner, got, dense):
    return pl.pallas_call(
        merge_kernel,
        out_shape=jax.ShapeDtypeStruct((NW, MROWS, EMB), BF16),
        in_specs=[SMEM] + [VMEM] * 2,
        out_specs=VMEM,
        scratch_shapes=[
            pltpu.VMEM((NW, MROWS, EMB), F32),
        ],
        compiler_params=params(),
        cost_estimate=cost(0),
        name="merge",
    )(owner, got, dense)


def split_kernel(got, rows, up, down, stage):
    for y in range(NY):
        one = got[y * NZ].astype(F32)
        for z in range(1, NZ):
            one = one + got[y * NZ + z].astype(F32)
        for n in range(NX * NC):
            rows[n, y * PIECE : (y + 1) * PIECE] = one[:PIECE]
        stage[y] = one[PIECE:] * (1.0 / math.sqrt(S * NW * NX * NC))
    for y in range(NY):
        for j in range(XB):
            at = (y * XB + j) * EMB
            if at < COLS * EMB:
                for g, to in enumerate((up, down)):
                    to[:, at : at + EMB] = stage[y, j * 4 + g * 2 : j * 4 + g * 2 + 2]


def split(got):
    grad = jax.ShapeDtypeStruct((2, COLS * EMB), F32)
    return pl.pallas_call(
        split_kernel,
        out_shape=(jax.ShapeDtypeStruct((NX * NC, ROWB, EMB), F32), grad, grad),
        in_specs=[VMEM],
        out_specs=(VMEM, VMEM, VMEM),
        scratch_shapes=[pltpu.VMEM((NY, MROWS - PIECE, EMB), F32)],
        compiler_params=params(),
        cost_estimate=cost(0),
        name="split",
    )(got)


def adagrad_rows(rows, accum, admitted, grad):
    begin_acc = jnp.where(admitted == 1, jnp.float32(0.1), accum)
    new_acc = begin_acc + jnp.mean(grad * grad, axis=1)
    new_values = rows - 0.5 * grad / (jnp.sqrt(new_acc)[:, None] + 1e-08)
    return (new_values, new_acc)


def local(
    cross_input,
    upstream,
    cross_down,
    cross_up,
    cross_bias,
    bag_rows,
    bag_lengths,
    table_owner,
    table_rows,
    row_accum,
    admitted,
):
    def send(a, axis, k):
        size = lax.axis_size(axis)
        return lax.ppermute(a, axis, [(i, (i + k) % size) for i in range(size)])

    pair, coded = pack(
        cross_input, upstream, jnp.transpose(bag_rows, (1, 2, 0)), bag_lengths.T
    )
    own = lax.all_to_all(pair, "y", split_axis=0, concat_axis=0, tiled=True)
    keep, give, *blocks = cross(
        cross_input, upstream, cross_down, cross_up, cross_bias, coded
    )
    low0 = jnp.stack([keep, send(give, "c", 1)])
    lows = [low0] + [send(low0, "y", k) for k in range(1, NY)]

    blocks = [blocks[0]] + [send(blocks[k], "x", k) for k in range(1, NX)]
    keep, give = bag_sums(blocks)
    sib = send(own, "c", 1)
    parts = dense_both(dense_own(own, lows), sib, lows)
    got = send(give, "c", 1)
    got, parts = lax.optimization_barrier((got, parts))
    parts = [parts[0]] + [send(parts[k], "x", k) for k in range(1, NX)]
    sums = bag_add(keep, got)
    got = lax.all_to_all(sums, ("y", "x"), split_axis=0, concat_axis=0, tiled=True)
    merged = merge(table_owner, got, across(parts))
    merged = lax.all_to_all(merged, WIDE, split_axis=0, concat_axis=0, tiled=True)
    rows, grad_up, grad_down = split(merged)
    rows = lax.all_to_all(rows, ("x", "c"), split_axis=0, concat_axis=0, tiled=True)
    new_rows, new_accum = adagrad_rows(
        table_rows, row_accum, admitted, rows.reshape(UNIQ, EMB)
    )
    return (new_rows, new_accum, grad_up, grad_down)


def solution(mesh):
    inner = Mesh(mesh.devices.reshape(NY, NZ, NX, NC), ALL)
    return jax.shard_map(
        local,
        mesh=inner,
        in_specs=(
            P(ALL, None),
            P(ALL, None),
            P(),
            P(),
            P(),
            P(ALL, None, None),
            P(ALL, None),
            P(),
            P(WIDE, None),
            P(WIDE),
            P(WIDE),
        ),
        out_specs=(
            P(WIDE, None),
            P(WIDE),
            P(ALL, None),
            P(ALL, None),
        ),
        check_vma=False,
    )
```

```python
import math

import jax
import jax.numpy as jnp
import numpy as np
from jax import lax
from jax.experimental import pallas as pl
from jax.experimental.pallas import tpu as pltpu
from jax.sharding import Mesh
from jax.sharding import PartitionSpec as P

NY, NZ, NX, NC = 4, 8, 4, 2
NW = NY * NZ
EMB, TABLES, RANK, UNIQ, BAG = 128, 26, 512, 512, 16
COLS = 27
XB = 7
S = 128
HALF = RANK // NC
ROWB = UNIQ // (NX * NC)
PIECE = ROWB // NY
DROWS = XB * 4
MROWS = 48
TX = 7
NONE = 256.0
F32, BF16 = jnp.float32, jnp.bfloat16
WIDE = ("y", "z")
ALL = ("y", "z", "x", "c")
VMEM = pl.BlockSpec(memory_space=pltpu.VMEM)
SMEM = pl.BlockSpec(memory_space=pltpu.SMEM)


def rank_order():
    order = np.arange(RANK).reshape(NY, NZ, NX, NC, 2).transpose(3, 2, 1, 0, 4).reshape(-1)
    return np.eye(RANK, dtype=np.float32)[order]


def params(mib=24):
    return pltpu.CompilerParams(vmem_limit_bytes=mib * 1024 * 1024)


def cost(us):
    return pl.CostEstimate(flops=int(us * 1e9), bytes_accessed=int(us * 1e5), transcendentals=0)


def axis(name):
    return lax.axis_index(name).astype(jnp.int32)


PACKS = 4


def pack_kernel(x_in, u_in, ids_in, lengths_in, pair, coded, x, u, ids, lengths, stage, in_sems, out_sems):
    rows = S // PACKS
    loads, stores = [], []
    for i in range(PACKS):
        at = pl.ds(i * rows, rows)
        loads.append(
            [
                pltpu.make_async_copy(x_in.at[at], x.at[at], in_sems.at[2 * i]),
                pltpu.make_async_copy(u_in.at[at], u.at[at], in_sems.at[2 * i + 1]),
            ]
        )
        stores.append(
            [
                pltpu.make_async_copy(
                    stage.at[b, :, at], pair.at[b, :, at], out_sems.at[i * NY + b]
                )
                for b in range(NY)
            ]
        )
    small = [
        pltpu.make_async_copy(ids_in, ids, in_sems.at[2 * PACKS]),
        pltpu.make_async_copy(lengths_in, lengths, in_sems.at[2 * PACKS + 1]),
    ]
    for copy in sum(loads, []) + small:
        copy.start()
    for i in range(PACKS):
        at = slice(i * rows, (i + 1) * rows)
        for copy in loads[i]:
            copy.wait()
        for b in range(NY):
            size = min(XB, COLS - b * XB) * EMB
            cols = slice(b * XB * EMB, b * XB * EMB + size)
            one = x[at, cols]
            stage[b, 0, at, :size] = (u[at, cols].astype(F32) * one.astype(F32)).astype(BF16)
            stage[b, 1, at, :size] = one
            if size < XB * EMB:
                stage[b, :, at, size:] = jnp.zeros((2, rows, XB * EMB - size), BF16)
            stores[i][b].start()
    for copy in small:
        copy.wait()
    position = lax.broadcasted_iota(jnp.int32, (BAG, S), 0)
    for t in range(TABLES):
        code = jnp.where(position < lengths[t : t + 1], (ids[t] - 256).astype(F32), NONE)
        coded[t] = code.astype(BF16)
    for copy in sum(stores, []):
        copy.wait()


def pack(x, u, ids, lengths):
    anywhere = pl.BlockSpec(memory_space=pl.ANY)
    shape = (NY, 2, S, XB * EMB)
    return pl.pallas_call(
        pack_kernel,
        out_shape=(
            jax.ShapeDtypeStruct(shape, BF16),
            jax.ShapeDtypeStruct((TABLES, BAG, S), BF16),
        ),
        in_specs=[anywhere] * 4,
        out_specs=(anywhere, VMEM),
        scratch_shapes=[
            pltpu.VMEM(x.shape, BF16),
            pltpu.VMEM(x.shape, BF16),
            pltpu.VMEM((TABLES, BAG, S), jnp.int32),
            pltpu.VMEM((TABLES, S), jnp.int32),
            pltpu.VMEM(shape, BF16),
            pltpu.SemaphoreType.DMA((2 * PACKS + 2,)),
            pltpu.SemaphoreType.DMA((PACKS * NY,)),
        ],
        compiler_params=params(60),
        cost_estimate=cost(1.5),
        name="pack",
    )(x, u, ids, lengths)


def cross_kernel(
    x_in, u_in, down_in, up_in, bias, order, coded, keep, give, out0, out1, out2, out3, x, u, down, up, pooled, sems
):
    spans = [(at, min(at + XB * EMB, COLS * EMB)) for at in range(0, COLS * EMB, XB * EMB)]
    first = [pltpu.make_async_copy(x_in, x, sems.at[0]), pltpu.make_async_copy(u_in, u, sems.at[1])]
    loads = []
    for w, (src, to) in enumerate(((down_in, down), (up_in, up))):
        loads.append([])
        for i, (begin, end) in enumerate(spans):
            at = pl.ds(begin, end - begin)
            loads[w].append(
                pltpu.make_async_copy(src.at[:, at], to.at[:, at], sems.at[2 + w * NY + i])
            )
    for copy in first[:1] + loads[0] + first[1:] + loads[1]:
        copy.start()

    def low_of(weight, copies, piece):
        total = jnp.zeros((RANK, S), F32)
        for copy, (begin, end) in zip(copies, spans):
            copy.wait()
            total = total + lax.dot_general(
                weight[:, begin:end], piece(begin, end), (((1,), (1,)), ((), ())), preferred_element_type=F32
            )
        return total.astype(BF16)

    first[0].wait()
    low = low_of(down, loads[0], lambda begin, end: x[:, begin:end])
    first[1].wait()
    d_low = low_of(
        up,
        loads[1],
        lambda begin, end: (u[:, begin:end].astype(F32) * x[:, begin:end].astype(F32)).astype(BF16),
    )
    for to, at in ((keep, axis("c")), (give, 1 - axis("c"))):
        pick = order[pl.ds(pl.multiple_of(at * HALF, HALF), HALF), :]
        for g, one in enumerate((low, d_low)):
            to[g] = jnp.dot(pick, one, preferred_element_type=F32).astype(BF16)
    low, d_low = low.T, d_low.T
    size = 2 * 256
    for at in range(EMB, COLS * EMB, size):
        cols = slice(at, min(at + size, COLS * EMB))
        scale = jnp.dot(low, up[:, cols], preferred_element_type=F32) + bias[cols].astype(F32)[None, :]
        back = jnp.dot(d_low, down[:, cols], preferred_element_type=F32)
        grad = u[:, cols].astype(F32) * (scale + 1.0) + back
        pooled[:, cols.start - EMB : cols.stop - EMB] = grad.astype(BF16)
    for k, out in enumerate((out0, out1, out2, out3)):
        to = lax.rem(axis("x") + k, NX)
        for i in range(TX):

            def put(out=out, to=to, i=i):
                t = to * TX + i
                out[i, :S] = pooled[:, pl.ds(pl.multiple_of(t * EMB, EMB), EMB)]
                out[i, S:] = coded[t]

            def blank(out=out, i=i):
                out[i, :S] = jnp.zeros((S, EMB), BF16)
                out[i, S:] = jnp.full((BAG, S), NONE, BF16)

            if (NX - 1) * TX + i < TABLES:
                put()
            else:
                pl.when(to < NX - 1)(put)
                pl.when(to == NX - 1)(blank)


def cross(x, u, down, up, bias, coded):
    half = jax.ShapeDtypeStruct((2, HALF, S), BF16)
    part = jax.ShapeDtypeStruct((TX, S + BAG, EMB), BF16)
    anywhere = pl.BlockSpec(memory_space=pl.ANY)
    return pl.pallas_call(
        cross_kernel,
        out_shape=(half, half) + (part,) * NX,
        in_specs=[anywhere] * 4 + [VMEM] * 3,
        out_specs=(VMEM,) * (2 + NX),
        scratch_shapes=[
            pltpu.VMEM(x.shape, BF16),
            pltpu.VMEM(x.shape, BF16),
            pltpu.VMEM(down.shape, BF16),
            pltpu.VMEM(down.shape, BF16),
            pltpu.VMEM((S, TABLES * EMB), BF16),
            pltpu.SemaphoreType.DMA((2 + 2 * NY,)),
        ],
        compiler_params=params(54),
        cost_estimate=cost(5),
        name="cross",
    )(x, u, down, up, bias, jnp.asarray(rank_order(), BF16), coded)


def bag_kernel(block0, block1, block2, block3, keep, give):
    blocks = (block0, block1, block2, block3)
    places = lax.broadcasted_iota(jnp.int32, (ROWB, NX * S), 0)

    @pl.loop(0, TX)
    def _(i):
        ids = jnp.concatenate([b[i, S:].astype(F32) for b in blocks], axis=1).astype(jnp.int32) + 256
        low = jnp.bitwise_and(ids, ROWB - 1)
        part = jnp.bitwise_and(lax.shift_right_arithmetic(ids, 6), 1)
        field = jnp.bitwise_and(lax.shift_right_arithmetic(ids, 7), 3)
        value = jnp.where(ids < UNIQ, lax.shift_left(jnp.ones_like(ids), field * 8), 0)
        grads = jnp.concatenate([b[i, :S] for b in blocks], axis=0)
        for out, mine in ((keep, axis("c")), (give, 1 - axis("c"))):
            worth = jnp.where(part == mine, value, 0)
            packed = jnp.zeros((ROWB, NX * S), jnp.int32)
            for j in range(BAG):
                packed = packed + jnp.where(places == low[j : j + 1], worth[j : j + 1], 0)
            counts = jnp.concatenate(
                [
                    jnp.bitwise_and(lax.shift_right_logical(packed, 8 * f), 255)
                    .astype(F32)
                    .astype(BF16)
                    for f in range(NX)
                ],
                axis=0,
            )
            out[i] = jnp.dot(counts, grads, preferred_element_type=F32).astype(out.dtype)


def bag_sums(blocks):
    shape = (TX, NX * ROWB, EMB)
    return pl.pallas_call(
        bag_kernel,
        out_shape=(jax.ShapeDtypeStruct(shape, F32), jax.ShapeDtypeStruct(shape, BF16)),
        in_specs=[VMEM] * NX,
        out_specs=(VMEM, VMEM),
        compiler_params=params(),
        cost_estimate=cost(10),
        name="bag_sums",
    )(*blocks)


def bag_add_kernel(keep, got, out):
    sums = (keep[...] + got[...].astype(F32)).astype(BF16)
    for k in range(NX):
        for m in range(NY):
            at = (k * NY + m) * PIECE
            out[m * NX + k] = sums[:, at : at + PIECE]


def bag_add(keep, got):
    return pl.pallas_call(
        bag_add_kernel,
        out_shape=jax.ShapeDtypeStruct((NY * NX, TX, PIECE, EMB), BF16),
        in_specs=[VMEM, VMEM],
        out_specs=VMEM,
        compiler_params=params(),
        cost_estimate=cost(0),
        name="bag_add",
    )(keep, got)


def gather_side(me_y, side, lows, ref, wide_x, wide_low):
    for g in range(2):
        for k in range(NY):
            src = lax.rem(me_y - k + NY, NY)
            wide_low[g, :, k * S : (k + 1) * S] = lows[k][side, g]
            wide_x[g, k * S : (k + 1) * S] = ref[src, g]


def dense_own_kernel(own, low0, low1, low2, low3, out, wide_x, wide_low):
    gather_side(axis("y"), 0, (low0, low1, low2, low3), own, wide_x, wide_low)
    for g in range(2):
        out[g] = jnp.dot(wide_low[g], wide_x[g], preferred_element_type=F32)


def dense_both_kernel(first, sib, low0, low1, low2, low3, out0, out1, out2, out3, wide_x, wide_low, stage):
    gather_side(axis("y"), 1, (low0, low1, low2, low3), sib, wide_x, wide_low)
    both = [
        first[g] + jnp.dot(wide_low[g], wide_x[g], preferred_element_type=F32) for g in range(2)
    ]
    for j in range(XB):
        pieces = [b[:, j * EMB : (j + 1) * EMB].reshape(NX, NZ, 8, EMB) for b in both]
        stage[:, :, j * 16 : (j + 1) * 16, :] = jnp.concatenate(pieces, axis=2).astype(BF16)

    for k, out in enumerate((out0, out1, out2, out3)):
        out[...] = stage[lax.rem(axis("x") + k, NX)]


WIDE_SIDE = [
    pltpu.VMEM((2, NY * S, XB * EMB), BF16),
    pltpu.VMEM((2, HALF, NY * S), BF16),
]


def dense_own(own, lows):
    return pl.pallas_call(
        dense_own_kernel,
        out_shape=jax.ShapeDtypeStruct((2, HALF, XB * EMB), F32),
        in_specs=[VMEM] * 5,
        out_specs=VMEM,
        scratch_shapes=WIDE_SIDE,
        compiler_params=params(),
        cost_estimate=cost(10),
        name="dense_own",
    )(own, *lows)


def dense_both(first, sib, lows):
    part = jax.ShapeDtypeStruct((NZ, 16 * XB, EMB), BF16)
    return pl.pallas_call(
        dense_both_kernel,
        out_shape=(part,) * NX,
        in_specs=[VMEM] * 6,
        out_specs=(VMEM,) * NX,
        scratch_shapes=WIDE_SIDE + [pltpu.VMEM((NX, NZ, 16 * XB, EMB), BF16)],
        compiler_params=params(),
        cost_estimate=cost(0),
        name="dense_both",
    )(first, sib, *lows)


def across_kernel(part0, part1, part2, part3, out):
    total = part0[...].astype(F32) + part1[...].astype(F32)
    out[...] = total + (part2[...].astype(F32) + part3[...].astype(F32))


def across(parts):
    return pl.pallas_call(
        across_kernel,
        out_shape=jax.ShapeDtypeStruct((NZ, 16 * XB, EMB), F32),
        in_specs=[VMEM] * NX,
        out_specs=VMEM,
        compiler_params=params(),
        cost_estimate=cost(10),
        name="across",
    )(*parts)


def merge_kernel(owner, got, dense, *refs):
    out, total = refs
    total[...] = jnp.zeros_like(total)

    for t in range(TABLES):
        x, i = t // TX, t % TX
        one = got[x, i].astype(F32)
        for y in range(1, NY):
            one = one + got[y * NX + x, i].astype(F32)
        to = owner[t]
        total[to, :PIECE] = total[to, :PIECE] + one

    for y in range(NY):
        for j in range(XB):
            for g in range(2):
                at, src = PIECE + j * 4 + g * 2, j * 16 + g * 8 + y * 2
                total[y * NZ : (y + 1) * NZ, at : at + 2] = dense[:, src : src + 2]
    out[...] = total[...].astype(BF16)


def merge(owner, got, dense):
    return pl.pallas_call(
        merge_kernel,
        out_shape=jax.ShapeDtypeStruct((NW, MROWS, EMB), BF16),
        in_specs=[SMEM] + [VMEM] * 2,
        out_specs=VMEM,
        scratch_shapes=[
            pltpu.VMEM((NW, MROWS, EMB), F32),
        ],
        compiler_params=params(),
        cost_estimate=cost(0),
        name="merge",
    )(owner, got, dense)


def split_kernel(got, rows, up, down, stage):
    for y in range(NY):
        one = got[y * NZ].astype(F32)
        for z in range(1, NZ):
            one = one + got[y * NZ + z].astype(F32)
        for n in range(NX * NC):
            rows[n, y * PIECE : (y + 1) * PIECE] = one[:PIECE]
        stage[y] = one[PIECE:] * (1.0 / math.sqrt(S * NW * NX * NC))
    for y in range(NY):
        for j in range(XB):
            at = (y * XB + j) * EMB
            if at < COLS * EMB:
                for g, to in enumerate((up, down)):
                    to[:, at : at + EMB] = stage[y, j * 4 + g * 2 : j * 4 + g * 2 + 2]


def split(got):
    grad = jax.ShapeDtypeStruct((2, COLS * EMB), F32)
    return pl.pallas_call(
        split_kernel,
        out_shape=(jax.ShapeDtypeStruct((NX * NC, ROWB, EMB), F32), grad, grad),
        in_specs=[VMEM],
        out_specs=(VMEM, VMEM, VMEM),
        scratch_shapes=[pltpu.VMEM((NY, MROWS - PIECE, EMB), F32)],
        compiler_params=params(),
        cost_estimate=cost(0),
        name="split",
    )(got)


def adagrad_rows(rows, accum, admitted, grad):
    begin_acc = jnp.where(admitted == 1, jnp.float32(0.1), accum)
    new_acc = begin_acc + jnp.mean(grad * grad, axis=1)
    new_values = rows - 0.5 * grad / (jnp.sqrt(new_acc)[:, None] + 1e-08)
    return (new_values, new_acc)


def local(
    cross_input,
    upstream,
    cross_down,
    cross_up,
    cross_bias,
    bag_rows,
    bag_lengths,
    table_owner,
    table_rows,
    row_accum,
    admitted,
):
    def send(a, axis, k):
        size = lax.axis_size(axis)
        return lax.ppermute(a, axis, [(i, (i + k) % size) for i in range(size)])

    pair, coded = pack(
        cross_input, upstream, jnp.transpose(bag_rows, (1, 2, 0)), bag_lengths.T
    )
    own = lax.all_to_all(pair, "y", split_axis=0, concat_axis=0, tiled=True)
    keep, give, *blocks = cross(
        cross_input, upstream, cross_down, cross_up, cross_bias, coded
    )
    low0 = jnp.stack([keep, send(give, "c", 1)])
    lows = [low0] + [send(low0, "y", k) for k in range(1, NY)]

    blocks = [blocks[0]] + [send(blocks[k], "x", k) for k in range(1, NX)]
    keep, give = bag_sums(blocks)
    sib = send(own, "c", 1)
    parts = dense_both(dense_own(own, lows), sib, lows)
    got = send(give, "c", 1)
    got, parts = lax.optimization_barrier((got, parts))
    parts = [parts[0]] + [send(parts[k], "x", k) for k in range(1, NX)]
    sums = bag_add(keep, got)
    got = lax.all_to_all(sums, ("y", "x"), split_axis=0, concat_axis=0, tiled=True)
    merged = merge(table_owner, got, across(parts))
    merged = lax.all_to_all(merged, WIDE, split_axis=0, concat_axis=0, tiled=True)
    rows, grad_up, grad_down = split(merged)
    rows = lax.all_to_all(rows, ("x", "c"), split_axis=0, concat_axis=0, tiled=True)
    new_rows, new_accum = adagrad_rows(
        table_rows, row_accum, admitted, rows.reshape(UNIQ, EMB)
    )
    return (new_rows, new_accum, grad_up, grad_down)


def solution(mesh):
    inner = Mesh(mesh.devices.reshape(NY, NZ, NX, NC), ALL)
    return jax.shard_map(
        local,
        mesh=inner,
        in_specs=(
            P(ALL, None),
            P(ALL, None),
            P(),
            P(),
            P(),
            P(ALL, None, None),
            P(ALL, None),
            P(),
            P(WIDE, None),
            P(WIDE),
            P(WIDE),
        ),
        out_specs=(
            P(WIDE, None),
            P(WIDE),
            P(ALL, None),
            P(ALL, None),
        ),
        check_vma=False,
    )
```
